32 devices in a mesh: parts: 2 (over y), src: 4 (over z), dst: 2 (over x), rep: 2 (over core).
Axes of the slice: x: 2, y: 2, z: 4, core: 2. Of those that a mesh axis runs over, the one named last changes fastest.
Arguments:
- edges: bfloat16 [8, 2, 2, 1024, 512], P(('parts', 'src'), 'dst', 'rep'), parts along dimension 0, may hold values from -6 to 6
- edge_count: int32 [8, 2, 2], P(('parts', 'src'), 'dst', 'rep'), parts along dimension 0, may hold values from 512 to 1024, as said below
- triplets: int32 [8, 2, 2, 3, 512], P(('parts', 'src'), 'dst', 'rep'), parts along dimension 0, may hold values from 0 to 63, as said below
- trip_count: int32 [8, 2, 2], P(('parts', 'src'), 'dst', 'rep'), parts along dimension 0, may hold values from 33 to 512, as said below
- rev_perm: int32 [8, 2, 2, 8], P(('parts', 'src'), 'dst', 'rep'), parts along dimension 0, may hold values from 0 to 7, each once within a row
- w_down: bfloat16 [512, 64], replicated, may hold values from -0.25 to 0.25
- w_up: bfloat16 [64, 512], replicated, may hold values from -0.25 to 0.25
- w_rev: bfloat16 [512, 512], replicated, may hold values from -0.25 to 0.25
- w_mlp1: bfloat16 [3, 512, 512], replicated, may hold values from -0.25 to 0.25
- w_mlp2: bfloat16 [3, 512, 512], replicated, may hold values from -0.25 to 0.25
- angular: bfloat16 [16, 128, 128], replicated, may hold values from -0.5 to 0.5
Outputs:
- updated: bfloat16 [8, 2, 2, 1024, 512], P(('parts', 'src'), 'dst', 'rep'), parts along dimension 0
The draws below stay inside these ranges and needn't reach their ends.
There are 2 independent parts, one for each index of `parts`. The reference program is written for one: setup_inputs(seed, part) draws one part's arguments, and reference() takes and returns one part's arrays. A program takes and returns all parts, laid end to end along the dimension named above; an argument that names none is the same for every part. Nothing has to cross between parts.
Inputs may be any that keep to these rules, and one draw needn't show every extreme that they name: `edge_count`: some device has exactly 1024 live edges in every draw. `triplets`: row 0 holds reader blocks below 16, row 1 source blocks, row 2 bases below 16; slots at or beyond trip_count hold arbitrary values of the same ranges. `trip_count`: some device has exactly 512 live triplet blocks in every draw; loads differ strongly between devices.
All inputs are finite; a program needn't handle non-finite values.
Results may differ from the reference program's by a relative error of at most 0.0067.
Values may be sent and summed in bfloat16 or wider, within the bound.
A program may use at most 64 MiB of HBM per device.

```python
import jax
import jax.numpy as jnp
from jax import lax

EMB = 512
TRIP_EMB = 64
BLK = 128
NB = 16
LAYERS = 3
E_DEV = 1024
TRIP_DEV = 512
BLK_DEV = 8
N_SRC = 4
N_DST = 2
N_REP = 2


def draw_edge_count(key, part):
    key = jax.random.fold_in(key, 11)
    first, second = jax.random.split(key)
    counts = jax.random.randint(first, (N_SRC * N_DST * N_REP,), E_DEV // 2, E_DEV + 1, dtype=jnp.int32)
    spot = jax.random.randint(second, (), 0, N_SRC * N_DST * N_REP, dtype=jnp.int32)
    counts = jnp.where(jnp.arange(N_SRC * N_DST * N_REP, dtype=jnp.int32) == spot, jnp.int32(E_DEV), counts)
    return counts.reshape(N_SRC, N_DST, N_REP)


def draw_trip_count(key, part):
    key = jax.random.fold_in(key, 23)
    first, second, third = jax.random.split(key, 3)
    total = N_SRC * N_DST * N_REP
    shifts = jax.random.randint(first, (total,), 0, 4, dtype=jnp.int32)
    jitter = jax.random.randint(second, (total,), 0, max(TRIP_DEV // 16, 1), dtype=jnp.int32)
    counts = jnp.right_shift(jnp.int32(TRIP_DEV), shifts) - jitter
    spot = jax.random.randint(third, (), 0, total, dtype=jnp.int32)
    counts = jnp.where(jnp.arange(total, dtype=jnp.int32) == spot, jnp.int32(TRIP_DEV), counts)
    return counts.reshape(N_SRC, N_DST, N_REP)


def draw_triplets(key, part):
    key = jax.random.fold_in(key, 37)
    first, second, third = jax.random.split(key, 3)
    shape = (N_SRC, N_DST, N_REP, TRIP_DEV)
    readers = jax.random.randint(first, shape, 0, N_REP * BLK_DEV, dtype=jnp.int32)
    sources = jax.random.randint(second, shape, 0, N_SRC * N_REP * BLK_DEV, dtype=jnp.int32)
    bases = jax.random.randint(third, shape, 0, NB, dtype=jnp.int32)
    return jnp.stack([readers, sources, bases], axis=3)


def steps_of(stream_key, dims, pieces, smallest, high):
    def one(position, parts):
        draws = jax.random.uniform(jax.random.fold_in(jax.random.fold_in(stream_key, 6), position), (parts,), jnp.float32, smallest / len(pieces), high / len(pieces))
        return jnp.repeat(jnp.exp(draws), dims[position] // parts).reshape((-1,) + (1,) * (len(dims) - position - 1))

    level = one(*pieces[0])
    for cut in pieces[1:]:
        level = level * one(*cut)
    return level


def gaussian(key, dims, spread, limit, cuts=(), kind=jnp.bfloat16):
    level = steps_of(key, dims, cuts, -0.22, 0.18) if cuts else 1.0
    drawn = jax.random.normal(key, dims, jnp.float32) * spread * level
    return jnp.minimum(jnp.maximum(drawn, -limit), limit).astype(kind)


def setup_inputs(seed: int = 0, part: int = 0) -> dict:
    keys = jax.random.split(jax.random.key(seed), 12)
    part_keys = jax.random.split(jax.random.fold_in(keys[11], part), 12)
    return {
        "edges": gaussian(part_keys[0], (N_SRC, N_DST, N_REP, E_DEV, EMB), 1.0, 6.0, ((0, 4), (1, 2), (2, 2))),
        "edge_count": draw_edge_count(jax.random.fold_in(jax.random.fold_in(keys[11], part), 71), part),
        "triplets": draw_triplets(jax.random.fold_in(jax.random.fold_in(keys[11], part), 71), part),
        "trip_count": draw_trip_count(jax.random.fold_in(jax.random.fold_in(keys[11], part), 71), part),
        "rev_perm": jax.vmap(lambda own: jax.random.permutation(own, BLK_DEV))(jax.random.split(part_keys[4], N_SRC * N_DST * N_REP)).reshape((N_SRC, N_DST, N_REP, BLK_DEV)).astype(jnp.int32),
        "w_down": gaussian(keys[5], (EMB, TRIP_EMB), EMB ** -0.5, 0.25),
        "w_up": gaussian(keys[6], (TRIP_EMB, EMB), (8 * TRIP_EMB) ** -0.5, 0.25),
        "w_rev": gaussian(keys[7], (EMB, EMB), EMB ** -0.5, 0.25),
        "w_mlp1": gaussian(keys[8], (LAYERS, EMB, EMB), EMB ** -0.5, 0.25),
        "w_mlp2": gaussian(keys[9], (LAYERS, EMB, EMB), EMB ** -0.5, 0.25),
        "angular": gaussian(keys[10], (NB, BLK, BLK), BLK ** -0.5, 0.5),
    }


root_three = 3.0 ** -0.5
root_two = 2.0 ** -0.5


def reference(edges, edge_count, triplets, trip_count, rev_perm, w_down, w_up, w_rev, w_mlp1, w_mlp2, angular):
    nblk = E_DEV // BLK
    live = jnp.arange(E_DEV, dtype=jnp.int32)[None, None, None, :] < edge_count[..., None]
    flat = edges.reshape(-1, EMB)
    proj = jax.nn.silu(jnp.dot(flat, w_down, preferred_element_type=jnp.float32))
    proj = proj.reshape(N_SRC, N_DST, N_REP, E_DEV, TRIP_EMB)
    proj = jnp.where(live[..., None], proj, jnp.float32(0.0)).astype(jnp.bfloat16)

    def pair(joint):
        s_idx = joint // N_DST
        d_idx = joint % N_DST
        blocks = proj[:, d_idx].reshape(N_SRC * N_REP * nblk, BLK, TRIP_EMB)
        acc = jnp.zeros((N_REP * nblk, BLK, TRIP_EMB), jnp.float32)
        for r_idx in range(N_REP):
            lists = triplets[s_idx, d_idx, r_idx]
            count = trip_count[s_idx, d_idx, r_idx]

            def add(total, step):
                term = jnp.dot(angular[lists[2, step]], blocks[lists[1, step]], preferred_element_type=jnp.float32)
                term = jnp.where(step < count, term, jnp.float32(0.0))
                return total.at[lists[0, step]].add(term), None

            acc, _ = lax.scan(add, acc, jnp.arange(TRIP_DEV, dtype=jnp.int32))
        return acc

    msg = lax.map(pair, jnp.arange(N_SRC * N_DST, dtype=jnp.int32))
    msg_b = msg.reshape(-1, E_DEV, TRIP_EMB).astype(jnp.bfloat16)
    mirror = edges[::-1, ::-1].reshape(-1, nblk, BLK, EMB)
    perms = rev_perm.reshape(-1, nblk)
    rev = jax.vmap(lambda blocks, order: blocks[order])(mirror, perms).reshape(-1, E_DEV, EMB)

    def tail(items):
        h_rows, m_rows, v_rows, l_rows = items
        trip = jax.nn.silu(jnp.dot(m_rows, w_up, preferred_element_type=jnp.float32))
        mixed = h_rows.astype(jnp.float32) + trip + jnp.dot(v_rows, w_rev, preferred_element_type=jnp.float32)
        state = (mixed * root_three).astype(jnp.bfloat16)
        for layer in range(LAYERS):
            hidden = jax.nn.silu(jnp.dot(state, w_mlp1[layer], preferred_element_type=jnp.float32)).astype(jnp.bfloat16)
            branch = jax.nn.silu(jnp.dot(hidden, w_mlp2[layer], preferred_element_type=jnp.float32))
            state = ((state.astype(jnp.float32) + branch) * root_two).astype(jnp.bfloat16)
        return jnp.where(l_rows[:, None], state, jnp.zeros_like(state))

    result = lax.map(tail, (edges.reshape(-1, E_DEV, EMB), msg_b, rev, live.reshape(-1, E_DEV)))
    return result.reshape(N_SRC, N_DST, N_REP, E_DEV, EMB)
```

```python
import jax
import jax.numpy as jnp
from jax import lax
from jax.sharding import PartitionSpec as P

root_three = 3.0 ** (-0.5)
root_two = 2.0 ** (-0.5)


def local(
    edges, edge_count, triplets, trip_count, rev_perm, w_down, w_up, w_rev, w_mlp1, w_mlp2, angular
):
    rows = edges.shape[3]
    width = edges.shape[4]
    blk = angular.shape[1]
    bases = angular.shape[0]
    trip_width = w_down.shape[1]
    nblk = rows // blk
    slots = triplets.shape[4]
    own_rows = edges.reshape(rows, width)
    n_src, n_dst = lax.axis_size("src"), lax.axis_size("dst")
    peers = n_src * n_dst
    mirror = [(q, peers - 1 - q) for q in range(peers)]
    partner = lax.ppermute(own_rows, ("src", "dst"), mirror)
    live = jnp.arange(rows, dtype=jnp.int32) < edge_count.reshape(())
    proj = jax.nn.silu(jnp.dot(own_rows, w_down, preferred_element_type=jnp.float32))
    proj = jnp.where(live[:, None], proj, jnp.float32(0.0)).astype(jnp.bfloat16)
    gathered = lax.all_gather(proj, ("src", "rep"), axis=0, tiled=True)
    blocks = gathered.reshape(-1, blk, trip_width)
    lists = triplets.reshape(3, slots)
    pair_size = lax.axis_size("rep")
    readers = pair_size * nblk
    valid = jnp.arange(slots, dtype=jnp.int32) < trip_count.reshape(())
    code = jnp.where(valid, lists[0] * bases + lists[2], -1)
    hot_code = (code[None, :] == jnp.arange(readers * bases, dtype=jnp.int32)[:, None]).astype(jnp.bfloat16)
    hot_source = (lists[1][None, :] == jnp.arange(blocks.shape[0], dtype=jnp.int32)[:, None]).astype(jnp.bfloat16)
    counts = lax.dot_general(hot_code, hot_source, (((1,), (1,)), ((), ())), preferred_element_type=jnp.float32)
    upper = jnp.floor(counts * (1.0 / 256.0)) * 256.0
    both = jnp.stack([(counts - upper), upper]).astype(jnp.bfloat16)
    sums = jnp.einsum("pxc,cjh->xjh", both, blocks, preferred_element_type=jnp.float32)
    sums = sums.reshape(readers, bases, blk, trip_width)
    high = sums.astype(jnp.bfloat16)
    low = (sums - high.astype(jnp.float32)).astype(jnp.bfloat16)
    msg = jnp.einsum("kij,pakjh->aih", angular, jnp.stack([high, low]), preferred_element_type=jnp.float32)
    msg = lax.psum_scatter(msg.reshape(readers, blk * trip_width), "rep", scatter_dimension=0, tiled=True)
    msg_b = msg.reshape(rows, trip_width).astype(jnp.bfloat16)
    trip = jax.nn.silu(jnp.dot(msg_b, w_up, preferred_element_type=jnp.float32))
    rev = partner.reshape(nblk, blk, width)[rev_perm.reshape(nblk)].reshape(rows, width)
    mixed = (
        own_rows.astype(jnp.float32)
        + trip
        + jnp.dot(rev, w_rev, preferred_element_type=jnp.float32)
    )
    state = (mixed * root_three).astype(jnp.bfloat16)
    for layer in range(w_mlp1.shape[0]):
        hidden = jax.nn.silu(
            jnp.dot(state, w_mlp1[layer], preferred_element_type=jnp.float32)
        ).astype(jnp.bfloat16)
        branch = jax.nn.silu(jnp.dot(hidden, w_mlp2[layer], preferred_element_type=jnp.float32))
        state = ((state.astype(jnp.float32) + branch) * root_two).astype(jnp.bfloat16)
    state = jnp.where(live[:, None], state, jnp.zeros_like(state))
    return state.reshape(1, 1, 1, rows, width)


def solution(mesh):
    in_specs = (
        P(("parts", "src"), "dst", "rep", None, None),
        P(("parts", "src"), "dst", "rep"),
        P(("parts", "src"), "dst", "rep", None, None),
        P(("parts", "src"), "dst", "rep"),
        P(("parts", "src"), "dst", "rep", None),
        P(),
        P(),
        P(),
        P(),
        P(),
        P(),
    )
    out_specs = P(("parts", "src"), "dst", "rep", None, None)
    return jax.shard_map(local, mesh=mesh, in_specs=in_specs, out_specs=out_specs, check_vma=False)
```

```python
import functools

import jax
import jax.numpy as jnp
from jax import lax
from jax.experimental import pallas as pl
from jax.experimental.pallas import tpu as pltpu
from jax.sharding import PartitionSpec as P

root_three = 3.0 ** (-0.5)
root_two = 2.0 ** (-0.5)
MESH = pl.DeviceIdType.MESH
HEAD = 3


def silu(v):
    return v * (0.5 + 0.5 * jnp.tanh(v * 0.5))


def mixed_dot(a, b, da, db):
    return lax.dot_general(a, b, (((da,), (db,)), ((), ())), preferred_element_type=jnp.float32)


def kernel(
    sizes, edge_count, trip_count, perm, lists, w_down, w_up, edges_in, rev_in, mlp1_in, mlp2_in, ang_in, out,
    edges, rev, w_rev, mlp1, mlp2, ang, acat, proj, gath, high, low, msg, part, give, take, pre, done,
    load_sem, bulk_send, bulk_recv, right_send, left_send, pair_send, gath_recv, msg_send, msg_recv,
):
    n_src, n_dst, n_rep = sizes
    s, d, r = lax.axis_index("src"), lax.axis_index("dst"), lax.axis_index("rep")
    rows, width = edges.shape
    bases, blk = ang.shape[0], ang.shape[1]
    nblk = rows // blk
    shift = nblk.bit_length() - 1
    trip_width = w_down.shape[1]
    slots = lists.shape[1]
    readers = n_rep * nblk
    codes = readers * bases
    mirror = {"src": n_src - 1 - s, "dst": n_dst - 1 - d}
    pair = {"rep": 1 - r}
    right = {"src": jnp.minimum(s + 1, n_src - 1)}
    left = {"src": jnp.maximum(s - 1, 0)}
    has_right, has_left = s + 1 < n_src, s > 0

    loads = [
        pltpu.make_async_copy(source, target, load_sem.at[index])
        for index, (source, target) in enumerate(
            [(edges_in, edges), (ang_in, ang), (rev_in, w_rev), (mlp1_in, mlp1), (mlp2_in, mlp2)]
        )
    ]
    for load in loads:
        load.start()

    barrier = pltpu.get_barrier_semaphore()
    pl.semaphore_signal(barrier, inc=1, device_id=mirror, device_id_type=MESH)
    pl.semaphore_signal(barrier, inc=1, device_id=pair, device_id_type=MESH)

    @pl.when(has_right)
    def _():
        pl.semaphore_signal(barrier, inc=1, device_id=right, device_id_type=MESH)

    @pl.when(has_left)
    def _():
        pl.semaphore_signal(barrier, inc=1, device_id=left, device_id_type=MESH)

    pl.semaphore_wait(barrier, 2 + has_right.astype(jnp.int32) + has_left.astype(jnp.int32))

    def bulk(m):
        span = pl.ds(pl.multiple_of(m * blk, blk), blk)
        return pltpu.make_async_remote_copy(
            src_ref=edges_in.at[span], dst_ref=rev.at[span],
            send_sem=bulk_send.at[m], recv_sem=bulk_recv.at[m], device_id=mirror, device_id_type=MESH,
        )

    def chunk(q, sems, o, target):
        return pltpu.make_async_remote_copy(
            src_ref=gath.at[q], dst_ref=gath.at[q],
            send_sem=sems.at[o], recv_sem=gath_recv.at[q], device_id=target, device_id_type=MESH,
        )

    for m in range(HEAD):
        bulk(m).start()

    loads[0].wait()
    lane = lax.broadcasted_iota(jnp.int32, (trip_width, blk), 1)
    down = w_down[...]
    for b in range(nblk):
        value = silu(mixed_dot(down, edges[b * blk:(b + 1) * blk, :], 0, 1))
        value = jnp.where(lane + b * blk < edge_count[0], value, 0.0)
        proj[pl.ds(b, trip_width, stride=nblk), :] = value
    own = s * n_rep + r
    gath[own] = proj[...].astype(jnp.bfloat16)
    chunk(own, pair_send, s, pair).start()

    @pl.when(has_right)
    def _():
        chunk(own, right_send, s, right).start()

    @pl.when(has_left)
    def _():
        chunk(own, left_send, s, left).start()

    for m in range(HEAD, nblk):
        bulk(m).start()

    loads[1].wait()
    for k in range(bases):
        acat[:, k * blk:(k + 1) * blk] = ang[k]
    a, c, k = lists[0:1, :], lists[1:2, :], lists[2:3, :]
    slot = lax.broadcasted_iota(jnp.int32, (1, slots), 1)
    code = jnp.where(slot < trip_count[0], k * readers + a, -1)
    hot_code = jnp.where(lax.broadcasted_iota(jnp.int32, (codes, slots), 0) == code, 1.0, 0.0).astype(jnp.bfloat16)
    cols = n_src * n_rep * nblk * 2
    line = lax.broadcasted_iota(jnp.int32, (cols, slots), 0)
    line = ((line >> (shift + 1)) << shift) + (line & (nblk - 1))
    hot_source = jnp.where(line == c, 1.0, 0.0).astype(jnp.bfloat16)
    counts = mixed_dot(hot_code, hot_source, 1, 1)
    odd = (lax.broadcasted_iota(jnp.int32, (codes, cols), 1) >> shift) & 1
    counts = jnp.concatenate([jnp.where(odd == 0, counts, 0.0), jnp.where(odd == 1, counts, 0.0)], axis=0)
    upper = jnp.floor(counts * (1.0 / 256.0)) * 256.0
    lower = (counts - upper).astype(jnp.bfloat16)
    upper = upper.astype(jnp.bfloat16)

    for hop in range(1, n_src):
        before, after = s - hop, s + hop

        @pl.when(before >= 0)
        def _():
            o = jnp.maximum(before, 0)
            q = o * n_rep + r
            chunk(q, left_send, o, left).wait_recv()

            @pl.when(has_right)
            def _():
                chunk(q, right_send, o, right).start()

            chunk(q, pair_send, o, pair).start()

        @pl.when(after < n_src)
        def _():
            o = jnp.minimum(after, n_src - 1)
            q = o * n_rep + r
            chunk(q, right_send, o, right).wait_recv()

            @pl.when(has_left)
            def _():
                chunk(q, left_send, o, left).start()

            chunk(q, pair_send, o, pair).start()

    for o in range(n_src):
        chunk(o * n_rep + 1 - r, pair_send, o, pair).wait_recv()

    def project(p, carry):
        halves = [
            gath[:, pl.ds(pl.multiple_of((2 * p + h) * 2 * nblk, 2 * nblk), 2 * nblk), :].reshape(cols, blk)
            for h in range(2)
        ]
        block = jnp.concatenate(halves, axis=1)
        sums = mixed_dot(lower, block, 1, 0) + mixed_dot(upper, block, 1, 0)
        first = sums.astype(jnp.bfloat16)
        second = (sums - first.astype(jnp.float32)).astype(jnp.bfloat16)
        for h in range(2):
            for odd_row in range(2):
                channel = (2 * p + h) * 2 + odd_row
                place = pl.ds(pl.multiple_of(channel * readers, readers), readers)
                for k in range(bases):
                    low_row = odd_row * codes + k * readers
                    high[place, k * blk:(k + 1) * blk] = first[low_row:low_row + readers, h * blk:(h + 1) * blk]
                    low[place, k * blk:(k + 1) * blk] = second[low_row:low_row + readers, h * blk:(h + 1) * blk]
        return carry

    lax.fori_loop(0, trip_width // 4, project, 0)

    span = 16
    for step in range(trip_width // span):
        place = slice(step * span * readers, (step + 1) * span * readers)
        total = mixed_dot(high[place, :], acat[...], 1, 1) + mixed_dot(low[place, :], acat[...], 1, 1)
        msg[step * span:(step + 1) * span] = total.reshape(span, readers, blk)
    mine = pl.ds(pl.multiple_of(r * nblk, nblk), nblk)
    other = pl.ds(pl.multiple_of((1 - r) * nblk, nblk), nblk)
    give[...] = msg[:, other, :].reshape(trip_width * nblk, blk)
    swap = pltpu.make_async_remote_copy(
        src_ref=give, dst_ref=take, send_sem=msg_send, recv_sem=msg_recv, device_id=pair, device_id_type=MESH,
    )
    swap.start()
    part[...] = msg[:, mine, :].reshape(trip_width * nblk, blk)
    swap.wait()
    part[...] = part[...] + take[...]
    for b in range(nblk):
        block = part[pl.ds(b, trip_width, stride=nblk), :].astype(jnp.bfloat16)
        trip = silu(mixed_dot(block, w_up[...], 0, 0))
        pre[b] = edges[b * blk:(b + 1) * blk, :].astype(jnp.float32) + trip

    for load in loads[2:]:
        load.wait()

    def tail(m, carry):
        bulk(m).wait_recv()
        b = jnp.int32(0)
        for j in range(nblk):
            b = jnp.where(perm[j] == m, j, b)
        span = pl.ds(pl.multiple_of(m * blk, blk), blk)
        state = ((pre[b] + mixed_dot(rev[span, :], w_rev[...], 1, 0)) * root_three).astype(jnp.bfloat16)
        for layer in range(mlp1.shape[0]):
            hidden = silu(mixed_dot(state, mlp1[layer], 1, 0)).astype(jnp.bfloat16)
            branch = silu(mixed_dot(hidden, mlp2[layer], 1, 0))
            state = ((state.astype(jnp.float32) + branch) * root_two).astype(jnp.bfloat16)
        done[m] = state
        return carry

    lax.fori_loop(0, nblk, tail, 0)

    line = lax.broadcasted_iota(jnp.int32, (blk, width), 0)
    for b in range(nblk):
        value = done[perm[b]]
        out[b * blk:(b + 1) * blk, :] = jnp.where(line + b * blk < edge_count[0], value, jnp.zeros_like(value))

    for m in range(nblk):
        bulk(m).wait_send()
    for o in range(n_src):
        chunk(o * n_rep + r, pair_send, o, pair).wait_send()

        @pl.when(jnp.logical_and(has_right, o <= s))
        def _():
            chunk(o * n_rep + r, right_send, o, right).wait_send()

        @pl.when(jnp.logical_and(has_left, o >= s))
        def _():
            chunk(o * n_rep + r, left_send, o, left).wait_send()


def solution(mesh):
    n_src, n_dst, n_rep = mesh.shape["src"], mesh.shape["dst"], mesh.shape["rep"]

    def local(edges, edge_count, triplets, trip_count, rev_perm, w_down, w_up, w_rev, w_mlp1, w_mlp2, angular):
        rows, width = edges.shape[3], edges.shape[4]
        bases, blk = angular.shape[0], angular.shape[1]
        nblk = rows // blk
        trip_width = w_down.shape[1]
        readers = n_rep * nblk
        kind, full = jnp.bfloat16, jnp.float32
        smem = pl.BlockSpec(memory_space=pltpu.SMEM)
        vmem = pl.BlockSpec(memory_space=pltpu.VMEM)
        hbm = pl.BlockSpec(memory_space=pl.ANY)
        dma = pltpu.SemaphoreType.DMA
        out = pl.pallas_call(
            functools.partial(kernel, (n_src, n_dst, n_rep)),
            out_shape=jax.ShapeDtypeStruct((rows, width), kind),
            in_specs=[smem] * 3 + [vmem] * 3 + [hbm] * 5,
            out_specs=vmem,
            scratch_shapes=[
                pltpu.VMEM((rows, width), kind),
                pltpu.VMEM((rows, width), kind),
                pltpu.VMEM(w_rev.shape, kind),
                pltpu.VMEM(w_mlp1.shape, kind),
                pltpu.VMEM(w_mlp2.shape, kind),
                pltpu.VMEM(angular.shape, kind),
                pltpu.VMEM((blk, bases * blk), kind),
                pltpu.VMEM((trip_width * nblk, blk), full),
                pltpu.VMEM((n_src * n_rep, trip_width * nblk, blk), kind),
                pltpu.VMEM((trip_width * readers, bases * blk), kind),
                pltpu.VMEM((trip_width * readers, bases * blk), kind),
                pltpu.VMEM((trip_width, readers, blk), full),
                pltpu.VMEM((trip_width * nblk, blk), full),
                pltpu.VMEM((trip_width * nblk, blk), full),
                pltpu.VMEM((trip_width * nblk, blk), full),
                pltpu.VMEM((nblk, blk, width), full),
                pltpu.VMEM((nblk, blk, width), kind),
                dma((5,)),
                dma((nblk,)),
                dma((nblk,)),
                dma((n_src,)),
                dma((n_src,)),
                dma((n_src,)),
                dma((n_src * n_rep,)),
                dma,
                dma,
            ],
            compiler_params=pltpu.CompilerParams(
                collective_id=0, has_side_effects=True, vmem_limit_bytes=48 << 20
            ),
        )(
            edge_count.reshape(1), trip_count.reshape(1), rev_perm.reshape(nblk), triplets.reshape(3, -1),
            w_down, w_up, edges.reshape(rows, width), w_rev, w_mlp1, w_mlp2, angular,
        )
        return out.reshape(1, 1, 1, rows, width)

    split = ("parts", "src"), "dst", "rep"
    in_specs = (
        P(*split, None, None),
        P(*split),
        P(*split, None, None),
        P(*split),
        P(*split, None),
    ) + (P(),) * 6
    return jax.shard_map(local, mesh=mesh, in_specs=in_specs, out_specs=P(*split, None, None), check_vma=False)
```

```python
import functools

import jax
import jax.numpy as jnp
from jax import lax
from jax.experimental import pallas as pl
from jax.experimental.pallas import tpu as pltpu
from jax.sharding import PartitionSpec as P

root_three = 3.0 ** (-0.5)
root_two = 2.0 ** (-0.5)
MESH = pl.DeviceIdType.MESH
PIECE = 64
HEAD = 2
GAP = 1
MIDDLE = 4
LATE = 2
FAST = False


def silu(v):
    return v * (0.5 + 0.5 * jnp.tanh(v * 0.5))


def mixed_dot(a, b, da, db):
    return lax.dot_general(a, b, (((da,), (db,)), ((), ())), preferred_element_type=jnp.float32)


def kernel(
    sizes, edge_count, trip_count, perm, lists, w_down, w_up, edges_in, rev_in, mlp1_in, mlp2_in, ang_in, out,
    edges, rev, w_rev, mlp1, mlp2, ang, acat, proj, gath, high, low, msg, part, give, take, pre, done,
    load_sem, bulk_send, bulk_recv, right_send, left_send, pair_send, gath_recv, msg_send, msg_recv,
):
    n_src, n_dst, n_rep = sizes
    s, d, r = lax.axis_index("src"), lax.axis_index("dst"), lax.axis_index("rep")
    rows, width = edges.shape
    bases, blk = ang.shape[0], ang.shape[1]
    nblk = rows // blk
    shift = nblk.bit_length() - 1
    trip_width = w_down.shape[1]
    slots = lists.shape[1]
    readers = n_rep * nblk
    codes = readers * bases
    mirror = {"src": n_src - 1 - s, "dst": n_dst - 1 - d}
    pair = {"rep": 1 - r}
    right = {"src": jnp.minimum(s + 1, n_src - 1)}
    left = {"src": jnp.maximum(s - 1, 0)}
    has_right, has_left = s + 1 < n_src, s > 0

    loads = [
        pltpu.make_async_copy(source, target, load_sem.at[index])
        for index, (source, target) in enumerate(
            [(edges_in, edges), (ang_in, ang), (rev_in, w_rev), (mlp1_in, mlp1), (mlp2_in, mlp2)]
        )
    ]
    for load in loads:
        load.start()

    barrier = pltpu.get_barrier_semaphore()
    pl.semaphore_signal(barrier, inc=1, device_id=mirror, device_id_type=MESH)
    pl.semaphore_signal(barrier, inc=1, device_id=pair, device_id_type=MESH)

    @pl.when(has_right)
    def _():
        pl.semaphore_signal(barrier, inc=1, device_id=right, device_id_type=MESH)

    @pl.when(has_left)
    def _():
        pl.semaphore_signal(barrier, inc=1, device_id=left, device_id_type=MESH)

    pl.semaphore_wait(barrier, 2 + has_right.astype(jnp.int32) + has_left.astype(jnp.int32))

    def bulk(m):
        span = pl.ds(pl.multiple_of(m * PIECE, PIECE), PIECE)
        source = edges if FAST else edges_in
        return pltpu.make_async_remote_copy(
            src_ref=source.at[span], dst_ref=rev.at[span],
            send_sem=bulk_send.at[m], recv_sem=bulk_recv.at[m], device_id=mirror, device_id_type=MESH,
        )

    def chunk(q, sems, o, target):
        return pltpu.make_async_remote_copy(
            src_ref=gath.at[q], dst_ref=gath.at[q],
            send_sem=sems.at[o], recv_sem=gath_recv.at[q], device_id=target, device_id_type=MESH,
        )

    pieces = rows // PIECE
    queue = list(range(pieces))

    def send(count):
        for m in queue[:count]:
            bulk(m).start()
        del queue[:count]

    if FAST:
        loads[0].wait()
    send(HEAD)
    if not FAST:
        loads[0].wait()
    lane = lax.broadcasted_iota(jnp.int32, (trip_width, blk), 1)
    down = w_down[...]
    for b in range(nblk):
        value = silu(mixed_dot(down, edges[b * blk:(b + 1) * blk, :], 0, 1))
        value = jnp.where(lane + b * blk < edge_count[0], value, 0.0)
        proj[pl.ds(b, trip_width, stride=nblk), :] = value
    own = s * n_rep + r
    gath[own] = proj[...].astype(jnp.bfloat16)
    chunk(own, pair_send, s, pair).start()

    @pl.when(has_right)
    def _():
        chunk(own, right_send, s, right).start()

    @pl.when(has_left)
    def _():
        chunk(own, left_send, s, left).start()

    send(GAP)
    loads[1].wait()
    for k in range(bases):
        acat[:, k * blk:(k + 1) * blk] = ang[k]
    a, c, k = lists[0:1, :], lists[1:2, :], lists[2:3, :]
    slot = lax.broadcasted_iota(jnp.int32, (1, slots), 1)
    code = jnp.where(slot < trip_count[0], k * readers + a, -1)
    hot_code = jnp.where(lax.broadcasted_iota(jnp.int32, (codes, slots), 0) == code, 1.0, 0.0).astype(jnp.bfloat16)
    cols = n_src * n_rep * nblk * 2
    line = lax.broadcasted_iota(jnp.int32, (cols, slots), 0)
    line = ((line >> (shift + 1)) << shift) + (line & (nblk - 1))
    hot_source = jnp.where(line == c, 1.0, 0.0).astype(jnp.bfloat16)
    counts = mixed_dot(hot_code, hot_source, 1, 1)
    odd = (lax.broadcasted_iota(jnp.int32, (codes, cols), 1) >> shift) & 1
    counts = jnp.concatenate([jnp.where(odd == 0, counts, 0.0), jnp.where(odd == 1, counts, 0.0)], axis=0)
    upper = jnp.floor(counts * (1.0 / 256.0)) * 256.0
    lower = (counts - upper).astype(jnp.bfloat16)
    upper = upper.astype(jnp.bfloat16)

    for hop in range(1, n_src):
        before, after = s - hop, s + hop

        @pl.when(before >= 0)
        def _():
            o = jnp.maximum(before, 0)
            q = o * n_rep + r
            chunk(q, left_send, o, left).wait_recv()

            @pl.when(has_right)
            def _():
                chunk(q, right_send, o, right).start()

            chunk(q, pair_send, o, pair).start()

        @pl.when(after < n_src)
        def _():
            o = jnp.minimum(after, n_src - 1)
            q = o * n_rep + r
            chunk(q, right_send, o, right).wait_recv()

            @pl.when(has_left)
            def _():
                chunk(q, left_send, o, left).start()

            chunk(q, pair_send, o, pair).start()

        if hop < n_src - 1:
            send(GAP)

    send(MIDDLE)
    for o in range(n_src):
        chunk(o * n_rep + 1 - r, pair_send, o, pair).wait_recv()

    def project(p, carry):
        halves = [
            gath[:, pl.ds(pl.multiple_of((2 * p + h) * 2 * nblk, 2 * nblk), 2 * nblk), :].reshape(cols, blk)
            for h in range(2)
        ]
        block = jnp.concatenate(halves, axis=1)
        sums = mixed_dot(lower, block, 1, 0) + mixed_dot(upper, block, 1, 0)
        first = sums.astype(jnp.bfloat16)
        second = (sums - first.astype(jnp.float32)).astype(jnp.bfloat16)
        for h in range(2):
            for odd_row in range(2):
                channel = (2 * p + h) * 2 + odd_row
                place = pl.ds(pl.multiple_of(channel * readers, readers), readers)
                for k in range(bases):
                    low_row = odd_row * codes + k * readers
                    high[place, k * blk:(k + 1) * blk] = first[low_row:low_row + readers, h * blk:(h + 1) * blk]
                    low[place, k * blk:(k + 1) * blk] = second[low_row:low_row + readers, h * blk:(h + 1) * blk]
        return carry

    lax.fori_loop(0, trip_width // 4, project, 0)
    send(LATE)

    span = 16
    for step in range(trip_width // span):
        place = slice(step * span * readers, (step + 1) * span * readers)
        total = mixed_dot(high[place, :], acat[...], 1, 1) + mixed_dot(low[place, :], acat[...], 1, 1)
        msg[step * span:(step + 1) * span] = total.reshape(span, readers, blk)
    mine = pl.ds(pl.multiple_of(r * nblk, nblk), nblk)
    other = pl.ds(pl.multiple_of((1 - r) * nblk, nblk), nblk)
    give[...] = msg[:, other, :].reshape(trip_width * nblk, blk)
    swap = pltpu.make_async_remote_copy(
        src_ref=give, dst_ref=take, send_sem=msg_send, recv_sem=msg_recv, device_id=pair, device_id_type=MESH,
    )
    swap.start()
    send(len(queue))
    part[...] = msg[:, mine, :].reshape(trip_width * nblk, blk)
    swap.wait()
    part[...] = part[...] + take[...]
    for b in range(nblk):
        block = part[pl.ds(b, trip_width, stride=nblk), :].astype(jnp.bfloat16)
        trip = silu(mixed_dot(block, w_up[...], 0, 0))
        pre[b] = edges[b * blk:(b + 1) * blk, :].astype(jnp.float32) + trip

    for load in loads[2:]:
        load.wait()

    def tail(m, carry):
        for j in range(blk // PIECE):
            bulk(m * (blk // PIECE) + j).wait_recv()
        b = jnp.int32(0)
        for j in range(nblk):
            b = jnp.where(perm[j] == m, j, b)
        span = pl.ds(pl.multiple_of(m * blk, blk), blk)
        state = ((pre[b] + mixed_dot(rev[span, :], w_rev[...], 1, 0)) * root_three).astype(jnp.bfloat16)
        for layer in range(mlp1.shape[0]):
            hidden = silu(mixed_dot(state, mlp1[layer], 1, 0)).astype(jnp.bfloat16)
            branch = silu(mixed_dot(hidden, mlp2[layer], 1, 0))
            state = ((state.astype(jnp.float32) + branch) * root_two).astype(jnp.bfloat16)
        done[m] = state
        return carry

    lax.fori_loop(0, nblk, tail, 0)

    line = lax.broadcasted_iota(jnp.int32, (blk, width), 0)
    for b in range(nblk):
        value = done[perm[b]]
        out[b * blk:(b + 1) * blk, :] = jnp.where(line + b * blk < edge_count[0], value, jnp.zeros_like(value))

    for m in range(pieces):
        bulk(m).wait_send()
    for o in range(n_src):
        chunk(o * n_rep + r, pair_send, o, pair).wait_send()

        @pl.when(jnp.logical_and(has_right, o <= s))
        def _():
            chunk(o * n_rep + r, right_send, o, right).wait_send()

        @pl.when(jnp.logical_and(has_left, o >= s))
        def _():
            chunk(o * n_rep + r, left_send, o, left).wait_send()


def solution(mesh):
    n_src, n_dst, n_rep = mesh.shape["src"], mesh.shape["dst"], mesh.shape["rep"]

    def local(edges, edge_count, triplets, trip_count, rev_perm, w_down, w_up, w_rev, w_mlp1, w_mlp2, angular):
        rows, width = edges.shape[3], edges.shape[4]
        bases, blk = angular.shape[0], angular.shape[1]
        nblk = rows // blk
        trip_width = w_down.shape[1]
        readers = n_rep * nblk
        kind, full = jnp.bfloat16, jnp.float32
        smem = pl.BlockSpec(memory_space=pltpu.SMEM)
        vmem = pl.BlockSpec(memory_space=pltpu.VMEM)
        hbm = pl.BlockSpec(memory_space=pl.ANY)
        dma = pltpu.SemaphoreType.DMA
        out = pl.pallas_call(
            functools.partial(kernel, (n_src, n_dst, n_rep)),
            out_shape=jax.ShapeDtypeStruct((rows, width), kind),
            in_specs=[smem] * 3 + [vmem] * 3 + [hbm] * 5,
            out_specs=vmem,
            scratch_shapes=[
                pltpu.VMEM((rows, width), kind),
                pltpu.VMEM((rows, width), kind),
                pltpu.VMEM(w_rev.shape, kind),
                pltpu.VMEM(w_mlp1.shape, kind),
                pltpu.VMEM(w_mlp2.shape, kind),
                pltpu.VMEM(angular.shape, kind),
                pltpu.VMEM((blk, bases * blk), kind),
                pltpu.VMEM((trip_width * nblk, blk), full),
                pltpu.VMEM((n_src * n_rep, trip_width * nblk, blk), kind),
                pltpu.VMEM((trip_width * readers, bases * blk), kind),
                pltpu.VMEM((trip_width * readers, bases * blk), kind),
                pltpu.VMEM((trip_width, readers, blk), full),
                pltpu.VMEM((trip_width * nblk, blk), full),
                pltpu.VMEM((trip_width * nblk, blk), full),
                pltpu.VMEM((trip_width * nblk, blk), full),
                pltpu.VMEM((nblk, blk, width), full),
                pltpu.VMEM((nblk, blk, width), kind),
                dma((5,)),
                dma((rows // PIECE,)),
                dma((rows // PIECE,)),
                dma((n_src,)),
                dma((n_src,)),
                dma((n_src,)),
                dma((n_src * n_rep,)),
                dma,
                dma,
            ],
            compiler_params=pltpu.CompilerParams(
                collective_id=0, has_side_effects=True, vmem_limit_bytes=48 << 20
            ),
        )(
            edge_count.reshape(1), trip_count.reshape(1), rev_perm.reshape(nblk), triplets.reshape(3, -1),
            w_down, w_up, edges.reshape(rows, width), w_rev, w_mlp1, w_mlp2, angular,
        )
        return out.reshape(1, 1, 1, rows, width)

    split = ("parts", "src"), "dst", "rep"
    in_specs = (
        P(*split, None, None),
        P(*split),
        P(*split, None, None),
        P(*split),
        P(*split, None),
    ) + (P(),) * 6
    return jax.shard_map(local, mesh=mesh, in_specs=in_specs, out_specs=P(*split, None, None), check_vma=False)
```

```python
import functools

import jax
import jax.numpy as jnp
from jax import lax
from jax.experimental import pallas as pl
from jax.experimental.pallas import tpu as pltpu
from jax.sharding import PartitionSpec as P

root_three = 3.0 ** (-0.5)
root_two = 2.0 ** (-0.5)
MESH = pl.DeviceIdType.MESH
PIECE = 64
HEAD = 2
GAP = 1
MIDDLE = 4
LATE = 2
FAST = False


def silu(v):
    return v * (0.5 + 0.5 * jnp.tanh(v * 0.5))


def mixed_dot(a, b, da, db):
    return lax.dot_general(a, b, (((da,), (db,)), ((), ())), preferred_element_type=jnp.float32)


def kernel(
    sizes, edge_count, trip_count, perm, lists_in, down_in, up_in, edges_in, rev_in, mlp1_in, mlp2_in, ang_in, out,
    lists, w_down, w_up, edges, rev, w_rev, mlp1, mlp2, ang, acat, proj, gath, high, low, msg, part, give, take, pre, done,
    load_sem, bulk_send, bulk_recv, right_send, left_send, pair_send, gath_recv, msg_send, msg_recv,
):
    n_src, n_dst, n_rep = sizes
    s, d, r = lax.axis_index("src"), lax.axis_index("dst"), lax.axis_index("rep")
    rows, width = edges.shape
    bases, blk = ang.shape[0], ang.shape[1]
    nblk = rows // blk
    shift = nblk.bit_length() - 1
    trip_width = w_down.shape[0]
    slots = lists.shape[2]
    readers = n_rep * nblk
    codes = readers * bases
    mirror = {"src": n_src - 1 - s, "dst": n_dst - 1 - d}
    pair = {"rep": 1 - r}
    right = {"src": jnp.minimum(s + 1, n_src - 1)}
    left = {"src": jnp.maximum(s - 1, 0)}
    has_right, has_left = s + 1 < n_src, s > 0

    loads = [
        pltpu.make_async_copy(source, target, load_sem.at[index])
        for index, (source, target) in enumerate(
            [
                (edges_in, edges), (down_in, w_down), (lists_in, lists), (ang_in, ang),
                (up_in, w_up), (rev_in, w_rev), (mlp1_in, mlp1), (mlp2_in, mlp2),
            ]
        )
    ]
    for load in loads:
        load.start()

    barrier = pltpu.get_barrier_semaphore()
    pl.semaphore_signal(barrier, inc=1, device_id=mirror, device_id_type=MESH)
    pl.semaphore_signal(barrier, inc=1, device_id=pair, device_id_type=MESH)

    @pl.when(has_right)
    def _():
        pl.semaphore_signal(barrier, inc=1, device_id=right, device_id_type=MESH)

    @pl.when(has_left)
    def _():
        pl.semaphore_signal(barrier, inc=1, device_id=left, device_id_type=MESH)

    pl.semaphore_wait(barrier, 2 + has_right.astype(jnp.int32) + has_left.astype(jnp.int32))

    def bulk(m):
        span = pl.ds(pl.multiple_of(m * PIECE, PIECE), PIECE)
        source = edges if FAST else edges_in
        return pltpu.make_async_remote_copy(
            src_ref=source.at[span], dst_ref=rev.at[span],
            send_sem=bulk_send.at[m], recv_sem=bulk_recv.at[m], device_id=mirror, device_id_type=MESH,
        )

    def chunk(q, sems, o, target):
        return pltpu.make_async_remote_copy(
            src_ref=gath.at[q], dst_ref=gath.at[q],
            send_sem=sems.at[o], recv_sem=gath_recv.at[q], device_id=target, device_id_type=MESH,
        )

    pieces = rows // PIECE
    queue = list(range(pieces))

    def send(count):
        for m in queue[:count]:
            bulk(m).start()
        del queue[:count]

    if FAST:
        loads[0].wait()
    send(HEAD)
    if not FAST:
        loads[0].wait()
    loads[1].wait()
    lane = lax.broadcasted_iota(jnp.int32, (trip_width, blk), 1)
    down = w_down[...]
    for b in range(nblk):
        value = silu(mixed_dot(down, edges[b * blk:(b + 1) * blk, :], 1, 1))
        value = jnp.where(lane + b * blk < edge_count[0, 0, 0], value, 0.0)
        proj[pl.ds(b, trip_width, stride=nblk), :] = value
    own = s * n_rep + r
    gath[own] = proj[...].astype(jnp.bfloat16)
    chunk(own, pair_send, s, pair).start()

    @pl.when(has_right)
    def _():
        chunk(own, right_send, s, right).start()

    @pl.when(has_left)
    def _():
        chunk(own, left_send, s, left).start()

    send(GAP)
    loads[2].wait()
    loads[3].wait()
    for k in range(bases):
        acat[:, k * blk:(k + 1) * blk] = ang[k]
    a, c, k = lists[0], lists[1], lists[2]
    slot = lax.broadcasted_iota(jnp.int32, (1, slots), 1)
    code = jnp.where(slot < trip_count[0, 0, 0], k * readers + a, -1)
    hot_code = jnp.where(lax.broadcasted_iota(jnp.int32, (codes, slots), 0) == code, 1.0, 0.0).astype(jnp.bfloat16)
    cols = n_src * n_rep * nblk * 2
    line = lax.broadcasted_iota(jnp.int32, (cols, slots), 0)
    line = ((line >> (shift + 1)) << shift) + (line & (nblk - 1))
    hot_source = jnp.where(line == c, 1.0, 0.0).astype(jnp.bfloat16)
    counts = mixed_dot(hot_code, hot_source, 1, 1)
    odd = (lax.broadcasted_iota(jnp.int32, (codes, cols), 1) >> shift) & 1
    counts = jnp.concatenate([jnp.where(odd == 0, counts, 0.0), jnp.where(odd == 1, counts, 0.0)], axis=0)
    upper = jnp.floor(counts * (1.0 / 256.0)) * 256.0
    lower = (counts - upper).astype(jnp.bfloat16)
    upper = upper.astype(jnp.bfloat16)

    for hop in range(1, n_src):
        before, after = s - hop, s + hop

        @pl.when(before >= 0)
        def _():
            o = jnp.maximum(before, 0)
            q = o * n_rep + r
            chunk(q, left_send, o, left).wait_recv()

            @pl.when(has_right)
            def _():
                chunk(q, right_send, o, right).start()

            chunk(q, pair_send, o, pair).start()

        @pl.when(after < n_src)
        def _():
            o = jnp.minimum(after, n_src - 1)
            q = o * n_rep + r
            chunk(q, right_send, o, right).wait_recv()

            @pl.when(has_left)
            def _():
                chunk(q, left_send, o, left).start()

            chunk(q, pair_send, o, pair).start()

        if hop < n_src - 1:
            send(GAP)

    send(MIDDLE)
    for o in range(n_src):
        chunk(o * n_rep + 1 - r, pair_send, o, pair).wait_recv()

    def project(p, carry):
        halves = [
            gath[:, pl.ds(pl.multiple_of((2 * p + h) * 2 * nblk, 2 * nblk), 2 * nblk), :].reshape(cols, blk)
            for h in range(2)
        ]
        block = jnp.concatenate(halves, axis=1)
        sums = mixed_dot(lower, block, 1, 0) + mixed_dot(upper, block, 1, 0)
        first = sums.astype(jnp.bfloat16)
        second = (sums - first.astype(jnp.float32)).astype(jnp.bfloat16)
        for h in range(2):
            for odd_row in range(2):
                channel = (2 * p + h) * 2 + odd_row
                place = pl.ds(pl.multiple_of(channel * readers, readers), readers)
                for k in range(bases):
                    low_row = odd_row * codes + k * readers
                    high[place, k * blk:(k + 1) * blk] = first[low_row:low_row + readers, h * blk:(h + 1) * blk]
                    low[place, k * blk:(k + 1) * blk] = second[low_row:low_row + readers, h * blk:(h + 1) * blk]
        return carry

    lax.fori_loop(0, trip_width // 4, project, 0)
    send(LATE)

    span = 16
    for step in range(trip_width // span):
        place = slice(step * span * readers, (step + 1) * span * readers)
        total = mixed_dot(high[place, :], acat[...], 1, 1) + mixed_dot(low[place, :], acat[...], 1, 1)
        msg[step * span:(step + 1) * span] = total.reshape(span, readers, blk)
    mine = pl.ds(pl.multiple_of(r * nblk, nblk), nblk)
    other = pl.ds(pl.multiple_of((1 - r) * nblk, nblk), nblk)
    give[...] = msg[:, other, :].reshape(trip_width * nblk, blk)
    swap = pltpu.make_async_remote_copy(
        src_ref=give, dst_ref=take, send_sem=msg_send, recv_sem=msg_recv, device_id=pair, device_id_type=MESH,
    )
    swap.start()
    send(len(queue))
    part[...] = msg[:, mine, :].reshape(trip_width * nblk, blk)
    swap.wait()
    part[...] = part[...] + take[...]
    loads[4].wait()
    for b in range(nblk):
        block = part[pl.ds(b, trip_width, stride=nblk), :].astype(jnp.bfloat16)
        trip = silu(mixed_dot(block, w_up[...], 0, 0))
        pre[b] = edges[b * blk:(b + 1) * blk, :].astype(jnp.float32) + trip

    for load in loads[5:]:
        load.wait()

    def tail(m, carry):
        for j in range(blk // PIECE):
            bulk(m * (blk // PIECE) + j).wait_recv()
        b = jnp.int32(0)
        for j in range(nblk):
            b = jnp.where(perm[0, 0, 0, j] == m, j, b)
        span = pl.ds(pl.multiple_of(m * blk, blk), blk)
        state = ((pre[b] + mixed_dot(rev[span, :], w_rev[...], 1, 0)) * root_three).astype(jnp.bfloat16)
        for layer in range(mlp1.shape[0]):
            hidden = silu(mixed_dot(state, mlp1[layer], 1, 0)).astype(jnp.bfloat16)
            branch = silu(mixed_dot(hidden, mlp2[layer], 1, 0))
            state = ((state.astype(jnp.float32) + branch) * root_two).astype(jnp.bfloat16)
        done[m] = state
        return carry

    lax.fori_loop(0, nblk, tail, 0)

    line = lax.broadcasted_iota(jnp.int32, (blk, width), 0)
    for b in range(nblk):
        value = done[perm[0, 0, 0, b]]
        out[b * blk:(b + 1) * blk, :] = jnp.where(line + b * blk < edge_count[0, 0, 0], value, jnp.zeros_like(value))

    for m in range(pieces):
        bulk(m).wait_send()
    for o in range(n_src):
        chunk(o * n_rep + r, pair_send, o, pair).wait_send()

        @pl.when(jnp.logical_and(has_right, o <= s))
        def _():
            chunk(o * n_rep + r, right_send, o, right).wait_send()

        @pl.when(jnp.logical_and(has_left, o >= s))
        def _():
            chunk(o * n_rep + r, left_send, o, left).wait_send()


def solution(mesh):
    n_src, n_dst, n_rep = mesh.shape["src"], mesh.shape["dst"], mesh.shape["rep"]

    def local(edges, edge_count, triplets, trip_count, rev_perm, w_down, w_up, w_rev, w_mlp1, w_mlp2, angular):
        rows, width = edges.shape[3], edges.shape[4]
        bases, blk = angular.shape[0], angular.shape[1]
        nblk = rows // blk
        trip_width = w_down.shape[1]
        readers = n_rep * nblk
        kind, full = jnp.bfloat16, jnp.float32
        smem = pl.BlockSpec(memory_space=pltpu.SMEM)
        vmem = pl.BlockSpec(memory_space=pltpu.VMEM)
        hbm = pl.BlockSpec(memory_space=pltpu.HBM)
        dma = pltpu.SemaphoreType.DMA
        out = pl.pallas_call(
            functools.partial(kernel, (n_src, n_dst, n_rep)),
            out_shape=jax.ShapeDtypeStruct((rows, width), kind),
            in_specs=[smem] * 3 + [hbm] * 8,
            out_specs=vmem,
            scratch_shapes=[
                pltpu.VMEM((3, 1, triplets.shape[4]), jnp.int32),
                pltpu.VMEM((trip_width, width), kind),
                pltpu.VMEM(w_up.shape, kind),
                pltpu.VMEM((rows, width), kind),
                pltpu.VMEM((rows, width), kind),
                pltpu.VMEM(w_rev.shape, kind),
                pltpu.VMEM(w_mlp1.shape, kind),
                pltpu.VMEM(w_mlp2.shape, kind),
                pltpu.VMEM(angular.shape, kind),
                pltpu.VMEM((blk, bases * blk), kind),
                pltpu.VMEM((trip_width * nblk, blk), full),
                pltpu.VMEM((n_src * n_rep, trip_width * nblk, blk), kind),
                pltpu.VMEM((trip_width * readers, bases * blk), kind),
                pltpu.VMEM((trip_width * readers, bases * blk), kind),
                pltpu.VMEM((trip_width, readers, blk), full),
                pltpu.VMEM((trip_width * nblk, blk), full),
                pltpu.VMEM((trip_width * nblk, blk), full),
                pltpu.VMEM((trip_width * nblk, blk), full),
                pltpu.VMEM((nblk, blk, width), full),
                pltpu.VMEM((nblk, blk, width), kind),
                dma((8,)),
                dma((rows // PIECE,)),
                dma((rows // PIECE,)),
                dma((n_src,)),
                dma((n_src,)),
                dma((n_src,)),
                dma((n_src * n_rep,)),
                dma,
                dma,
            ],
            compiler_params=pltpu.CompilerParams(
                collective_id=0, has_side_effects=True, vmem_limit_bytes=60 << 20
            ),
        )(
            edge_count, trip_count, rev_perm, triplets.reshape(3, 1, -1),
            w_down.T, w_up, edges.reshape(rows, width), w_rev, w_mlp1, w_mlp2, angular,
        )
        return out.reshape(1, 1, 1, rows, width)

    split = ("parts", "src"), "dst", "rep"
    in_specs = (
        P(*split, None, None),
        P(*split),
        P(*split, None, None),
        P(*split),
        P(*split, None),
    ) + (P(),) * 6
    return jax.shard_map(local, mesh=mesh, in_specs=in_specs, out_specs=P(*split, None, None), check_vma=False)
```

```python
import functools

import jax
import jax.numpy as jnp
from jax import lax
from jax.experimental import pallas as pl
from jax.experimental.pallas import tpu as pltpu
from jax.sharding import PartitionSpec as P

root_three = 3.0 ** (-0.5)
root_two = 2.0 ** (-0.5)
MESH = pl.DeviceIdType.MESH
PIECE = 64
HEAD = 2
GAP = 1
MIDDLE = 4
LATE = 2
FAST = False


def silu(v):
    return v * (0.5 + 0.5 * jnp.tanh(v * 0.5))


def mixed_dot(a, b, da, db):
    return lax.dot_general(a, b, (((da,), (db,)), ((), ())), preferred_element_type=jnp.float32)


def kernel(
    sizes, edge_count, trip_count, perm, lists_in, down_in, up_in, edges_in, rev_in, mlp1_in, mlp2_in, ang_in, out,
    lists, w_down, w_up, edges, rev, w_rev, mlp1, mlp2, ang, acat, proj, gath, high, low, msg, part, give, take, pre, done,
    load_sem, bulk_send, bulk_recv, right_send, left_send, pair_send, gath_recv, msg_send, msg_recv,
):
    n_src, n_dst, n_rep = sizes
    s, d, r = lax.axis_index("src"), lax.axis_index("dst"), lax.axis_index("rep")
    rows, width = edges.shape
    bases, blk = ang.shape[0], ang.shape[1]
    nblk = rows // blk
    shift = nblk.bit_length() - 1
    trip_width = w_down.shape[0]
    slots = lists.shape[2]
    readers = n_rep * nblk
    codes = readers * bases
    mirror = {"src": n_src - 1 - s, "dst": n_dst - 1 - d}
    pair = {"rep": 1 - r}
    right = {"src": jnp.minimum(s + 1, n_src - 1)}
    left = {"src": jnp.maximum(s - 1, 0)}
    has_right, has_left = s + 1 < n_src, s > 0

    loads = [
        pltpu.make_async_copy(source, target, load_sem.at[index])
        for index, (source, target) in enumerate(
            [
                (edges_in, edges), (down_in, w_down), (lists_in, lists), (ang_in, ang),
                (up_in, w_up), (rev_in, w_rev), (mlp1_in, mlp1), (mlp2_in, mlp2),
            ]
        )
    ]
    for load in loads:
        load.start()

    barrier = pltpu.get_barrier_semaphore()
    pl.semaphore_signal(barrier, inc=1, device_id=mirror, device_id_type=MESH)
    pl.semaphore_signal(barrier, inc=1, device_id=pair, device_id_type=MESH)

    @pl.when(has_right)
    def _():
        pl.semaphore_signal(barrier, inc=1, device_id=right, device_id_type=MESH)

    @pl.when(has_left)
    def _():
        pl.semaphore_signal(barrier, inc=1, device_id=left, device_id_type=MESH)

    pl.semaphore_wait(barrier, 2 + has_right.astype(jnp.int32) + has_left.astype(jnp.int32))

    def bulk(m):
        span = pl.ds(pl.multiple_of(m * PIECE, PIECE), PIECE)
        source = edges if FAST else edges_in
        return pltpu.make_async_remote_copy(
            src_ref=source.at[span], dst_ref=rev.at[span],
            send_sem=bulk_send.at[m], recv_sem=bulk_recv.at[m], device_id=mirror, device_id_type=MESH,
        )

    def chunk(q, sems, o, target):
        return pltpu.make_async_remote_copy(
            src_ref=gath.at[q], dst_ref=gath.at[q],
            send_sem=sems.at[o], recv_sem=gath_recv.at[q], device_id=target, device_id_type=MESH,
        )

    pieces = rows // PIECE
    queue = list(range(pieces))

    def send(count):
        for m in queue[:count]:
            bulk(m).start()
        del queue[:count]

    if FAST:
        loads[0].wait()
    send(HEAD)
    if not FAST:
        loads[0].wait()
    loads[1].wait()
    lane = lax.broadcasted_iota(jnp.int32, (trip_width, blk), 1)
    down = w_down[...]
    for b in range(nblk):
        value = silu(mixed_dot(down, edges[b * blk:(b + 1) * blk, :], 1, 1))
        value = jnp.where(lane + b * blk < edge_count[0, 0, 0], value, 0.0)
        proj[pl.ds(b, trip_width, stride=nblk), :] = value
    own = s * n_rep + r
    gath[own] = proj[...].astype(jnp.bfloat16)
    chunk(own, pair_send, s, pair).start()

    @pl.when(has_right)
    def _():
        chunk(own, right_send, s, right).start()

    @pl.when(has_left)
    def _():
        chunk(own, left_send, s, left).start()

    send(GAP)
    loads[2].wait()
    loads[3].wait()
    for k in range(bases):
        acat[:, k * blk:(k + 1) * blk] = ang[k]
    a, c, k = lists[0], lists[1], lists[2]
    slot = lax.broadcasted_iota(jnp.int32, (1, slots), 1)
    code = jnp.where(slot < trip_count[0, 0, 0], k * readers + a, -1)
    hot_code = jnp.where(lax.broadcasted_iota(jnp.int32, (codes, slots), 0) == code, 1.0, 0.0).astype(jnp.bfloat16)
    cols = n_src * n_rep * nblk * 2
    line = lax.broadcasted_iota(jnp.int32, (cols, slots), 0)
    line = ((line >> (shift + 1)) << shift) + (line & (nblk - 1))
    hot_source = jnp.where(line == c, 1.0, 0.0).astype(jnp.bfloat16)
    counts = mixed_dot(hot_code, hot_source, 1, 1)
    odd = (lax.broadcasted_iota(jnp.int32, (codes, cols), 1) >> shift) & 1
    counts = jnp.concatenate([jnp.where(odd == 0, counts, 0.0), jnp.where(odd == 1, counts, 0.0)], axis=0)
    upper = jnp.floor(counts * (1.0 / 256.0)) * 256.0
    lower = (counts - upper).astype(jnp.bfloat16)
    upper = upper.astype(jnp.bfloat16)

    for hop in range(1, n_src):
        before, after = s - hop, s + hop

        @pl.when(before >= 0)
        def _():
            o = jnp.maximum(before, 0)
            q = o * n_rep + r
            chunk(q, left_send, o, left).wait_recv()

            @pl.when(has_right)
            def _():
                chunk(q, right_send, o, right).start()

            chunk(q, pair_send, o, pair).start()

        @pl.when(after < n_src)
        def _():
            o = jnp.minimum(after, n_src - 1)
            q = o * n_rep + r
            chunk(q, right_send, o, right).wait_recv()

            @pl.when(has_left)
            def _():
                chunk(q, left_send, o, left).start()

            chunk(q, pair_send, o, pair).start()

        if hop < n_src - 1:
            send(GAP)

    send(MIDDLE)
    for o in range(n_src):
        chunk(o * n_rep + 1 - r, pair_send, o, pair).wait_recv()

    def project(p, carry):
        halves = [
            gath[:, pl.ds(pl.multiple_of((2 * p + h) * 2 * nblk, 2 * nblk), 2 * nblk), :].reshape(cols, blk)
            for h in range(2)
        ]
        block = jnp.concatenate(halves, axis=1)
        sums = mixed_dot(lower, block, 1, 0) + mixed_dot(upper, block, 1, 0)
        first = sums.astype(jnp.bfloat16)
        second = (sums - first.astype(jnp.float32)).astype(jnp.bfloat16)
        for h in range(2):
            for odd_row in range(2):
                channel = (2 * p + h) * 2 + odd_row
                place = pl.ds(pl.multiple_of(channel * readers, readers), readers)
                for k in range(bases):
                    low_row = odd_row * codes + k * readers
                    high[place, k * blk:(k + 1) * blk] = first[low_row:low_row + readers, h * blk:(h + 1) * blk]
                    low[place, k * blk:(k + 1) * blk] = second[low_row:low_row + readers, h * blk:(h + 1) * blk]
        return carry

    lax.fori_loop(0, trip_width // 4, project, 0)
    send(LATE)

    span = 16
    for step in range(trip_width // span):
        place = slice(step * span * readers, (step + 1) * span * readers)
        total = mixed_dot(high[place, :], acat[...], 1, 1) + mixed_dot(low[place, :], acat[...], 1, 1)
        msg[step * span:(step + 1) * span] = total.reshape(span, readers, blk)
    mine = pl.ds(pl.multiple_of(r * nblk, nblk), nblk)
    other = pl.ds(pl.multiple_of((1 - r) * nblk, nblk), nblk)
    give[...] = msg[:, other, :].reshape(trip_width * nblk, blk)
    swap = pltpu.make_async_remote_copy(
        src_ref=give, dst_ref=take, send_sem=msg_send, recv_sem=msg_recv, device_id=pair, device_id_type=MESH,
    )
    swap.start()
    send(len(queue))
    part[...] = msg[:, mine, :].reshape(trip_width * nblk, blk)
    swap.wait()
    part[...] = part[...] + take[...]
    loads[4].wait()
    for b in range(nblk):
        block = part[pl.ds(b, trip_width, stride=nblk), :].astype(jnp.bfloat16)
        trip = silu(mixed_dot(block, w_up[...], 0, 0))
        pre[b] = edges[b * blk:(b + 1) * blk, :].astype(jnp.float32) + trip

    for load in loads[5:]:
        load.wait()

    def tail(m, carry):
        for j in range(blk // PIECE):
            bulk(m * (blk // PIECE) + j).wait_recv()
        b = jnp.int32(0)
        for j in range(nblk):
            b = jnp.where(perm[0, 0, 0, j] == m, j, b)
        half = blk // 2
        states = []
        for side in range(2):
            span = pl.ds(pl.multiple_of(m * blk + side * half, half), half)
            mixed = pre[b, side * half:(side + 1) * half] + mixed_dot(rev[span, :], w_rev[...], 1, 0)
            states.append((mixed * root_three).astype(jnp.bfloat16))
        for layer in range(mlp1.shape[0]):
            hidden = [silu(mixed_dot(state, mlp1[layer], 1, 0)).astype(jnp.bfloat16) for state in states]
            branches = [silu(mixed_dot(value, mlp2[layer], 1, 0)) for value in hidden]
            states = [
                ((state.astype(jnp.float32) + branch) * root_two).astype(jnp.bfloat16)
                for state, branch in zip(states, branches)
            ]
        done[m] = jnp.concatenate(states, axis=0)
        return carry

    lax.fori_loop(0, nblk, tail, 0)

    line = lax.broadcasted_iota(jnp.int32, (blk, width), 0)
    for b in range(nblk):
        value = done[perm[0, 0, 0, b]]
        out[b * blk:(b + 1) * blk, :] = jnp.where(line + b * blk < edge_count[0, 0, 0], value, jnp.zeros_like(value))

    for m in range(pieces):
        bulk(m).wait_send()
    for o in range(n_src):
        chunk(o * n_rep + r, pair_send, o, pair).wait_send()

        @pl.when(jnp.logical_and(has_right, o <= s))
        def _():
            chunk(o * n_rep + r, right_send, o, right).wait_send()

        @pl.when(jnp.logical_and(has_left, o >= s))
        def _():
            chunk(o * n_rep + r, left_send, o, left).wait_send()


def solution(mesh):
    n_src, n_dst, n_rep = mesh.shape["src"], mesh.shape["dst"], mesh.shape["rep"]

    def local(edges, edge_count, triplets, trip_count, rev_perm, w_down, w_up, w_rev, w_mlp1, w_mlp2, angular):
        rows, width = edges.shape[3], edges.shape[4]
        bases, blk = angular.shape[0], angular.shape[1]
        nblk = rows // blk
        trip_width = w_down.shape[1]
        readers = n_rep * nblk
        kind, full = jnp.bfloat16, jnp.float32
        smem = pl.BlockSpec(memory_space=pltpu.SMEM)
        vmem = pl.BlockSpec(memory_space=pltpu.VMEM)
        hbm = pl.BlockSpec(memory_space=pltpu.HBM)
        dma = pltpu.SemaphoreType.DMA
        out = pl.pallas_call(
            functools.partial(kernel, (n_src, n_dst, n_rep)),
            out_shape=jax.ShapeDtypeStruct((rows, width), kind),
            in_specs=[smem] * 3 + [hbm] * 8,
            out_specs=vmem,
            scratch_shapes=[
                pltpu.VMEM((3, 1, triplets.shape[4]), jnp.int32),
                pltpu.VMEM((trip_width, width), kind),
                pltpu.VMEM(w_up.shape, kind),
                pltpu.VMEM((rows, width), kind),
                pltpu.VMEM((rows, width), kind),
                pltpu.VMEM(w_rev.shape, kind),
                pltpu.VMEM(w_mlp1.shape, kind),
                pltpu.VMEM(w_mlp2.shape, kind),
                pltpu.VMEM(angular.shape, kind),
                pltpu.VMEM((blk, bases * blk), kind),
                pltpu.VMEM((trip_width * nblk, blk), full),
                pltpu.VMEM((n_src * n_rep, trip_width * nblk, blk), kind),
                pltpu.VMEM((trip_width * readers, bases * blk), kind),
                pltpu.VMEM((trip_width * readers, bases * blk), kind),
                pltpu.VMEM((trip_width, readers, blk), full),
                pltpu.VMEM((trip_width * nblk, blk), full),
                pltpu.VMEM((trip_width * nblk, blk), full),
                pltpu.VMEM((trip_width * nblk, blk), full),
                pltpu.VMEM((nblk, blk, width), full),
                pltpu.VMEM((nblk, blk, width), kind),
                dma((8,)),
                dma((rows // PIECE,)),
                dma((rows // PIECE,)),
                dma((n_src,)),
                dma((n_src,)),
                dma((n_src,)),
                dma((n_src * n_rep,)),
                dma,
                dma,
            ],
            compiler_params=pltpu.CompilerParams(
                collective_id=0, has_side_effects=True, vmem_limit_bytes=60 << 20
            ),
        )(
            edge_count, trip_count, rev_perm, triplets.reshape(3, 1, -1),
            w_down.T, w_up, edges.reshape(rows, width), w_rev, w_mlp1, w_mlp2, angular,
        )
        return out.reshape(1, 1, 1, rows, width)

    split = ("parts", "src"), "dst", "rep"
    in_specs = (
        P(*split, None, None),
        P(*split),
        P(*split, None, None),
        P(*split),
        P(*split, None),
    ) + (P(),) * 6
    return jax.shard_map(local, mesh=mesh, in_specs=in_specs, out_specs=P(*split, None, None), check_vma=False)
```
